256 devices in a mesh: blk: 8 (over z), uly: 32 (over x, y, core).
Axes of the slice: x: 4, y: 4, z: 8, core: 2. Of those that a mesh axis runs over, the one named last changes fastest.
Arguments:
- queries: bfloat16 [16384, 4096], P(('blk', 'uly')), may hold values from -120 to 120
- keys: bfloat16 [16384, 4096], P(('blk', 'uly')), may hold values from -30 to 30
- values: bfloat16 [16384, 4096], P(('blk', 'uly')), may hold values from -6 to 6
Outputs:
- attended: bfloat16 [16384, 4096], P(('blk', 'uly'))
- key_cache: bfloat16 [16384, 4096], P(('blk', 'uly'))
The draws below stay inside these ranges and needn't reach their ends.
All inputs are finite; a program needn't handle non-finite values.
Results may differ from the reference program's by a relative error of at most 0.0069.
Values may be sent and summed in bfloat16 or wider, within the bound.
No kernel may reach another device: no remote copies, remote signals or barrier semaphores. Data moves between devices by JAX's collectives and lax.ppermute only.
A program may use at most 64 MiB of HBM per device.

```python
import math
import jax
import jax.numpy as jnp
from jax import lax

HEADS = 32
HD = 128
D = 4096
TOKENS = 16384


def shared_keys(key):
    noise = jax.random.normal(jax.random.fold_in(key, 101), (TOKENS, D), jnp.float32)
    noise = jnp.clip(noise, -4.0, 4.0)
    rows = jnp.arange(TOKENS, dtype=jnp.int32)
    marked = rows % 512 == 505
    noise = jnp.where((marked & (rows > 0))[:, None], noise, noise)
    offset = 2.0 * jnp.clip(jax.random.normal(jax.random.fold_in(key, 102), (D,), jnp.float32), -3.0, 3.0)
    ramp = 1.0 + 2.0 * jnp.arange(TOKENS, dtype=jnp.float32) / TOKENS
    return noise + ramp[:, None] * offset[None, :]


def draw_keys(key, part):
    whole = shared_keys(key)
    return jnp.clip(whole, -30.0, 30.0).astype(jnp.bfloat16)


def draw_queries(key, part):
    key = jax.random.fold_in(key, 5)
    base = jax.random.normal(key, (TOKENS, D), jnp.float32)
    return jnp.clip(base, -120.0, 120.0).astype(jnp.bfloat16)


def level_of(own_key, shape, cuts, low, high):
    level, own = 1.0, jax.random.fold_in(own_key, 6)
    for position, shards_of in cuts:
        draws = jnp.exp(jax.random.uniform(jax.random.fold_in(own, position), (shards_of,), jnp.float32, low / len(cuts), high / len(cuts)))
        level = level * jnp.repeat(draws, shape[position] // shards_of).reshape([-1 if axis == position else 1 for axis in range(len(shape))])
    return level


def gaussian(stream_key, extent, deviation, reach, cuts=(), held_as=jnp.bfloat16):
    loudness = level_of(stream_key, extent, cuts, -0.22, 0.18) if cuts else 1.0
    result = jax.random.normal(stream_key, extent, jnp.float32) * deviation * loudness
    return jnp.minimum(jnp.maximum(result, -reach), reach).astype(held_as)


def setup_inputs(seed: int = 0) -> dict:
    key_list = jax.random.split(jax.random.key(seed), 4)
    queries = draw_queries(jax.random.fold_in(key_list[3], 71), 0)
    keys = draw_keys(jax.random.fold_in(key_list[3], 71), 0)
    values = gaussian(key_list[2], (TOKENS, D), 1.0, 6.0, ((0, 256),))
    return dict(queries=queries, keys=keys, values=values)


def reference(queries, keys, values):
    keys32 = keys.astype(jnp.float32)
    key_mean = lax.optimization_barrier(jnp.sum(keys32, axis=0)) / TOKENS
    key_cache = (keys32 - key_mean).astype(jnp.bfloat16)
    block = math.gcd(TOKENS, 512)
    count = TOKENS // block
    scale = 1.0 / math.sqrt(HD)
    q_heads = queries.reshape(TOKENS, HEADS, HD).transpose(1, 0, 2)
    k_heads = key_cache.reshape(TOKENS, HEADS, HD).transpose(1, 0, 2)
    v_heads = values.reshape(TOKENS, HEADS, HD).transpose(1, 0, 2)

    def one_head(operands):
        q_head, k_head, v_head = operands

        def one_block(index):
            q_block = lax.dynamic_slice_in_dim(q_head, index * block, block, 0)
            q_pos = index * block + jnp.arange(block, dtype=jnp.int32)

            def absorb(step, carry):
                run_max, run_sum, accum = carry
                k_block = lax.dynamic_slice_in_dim(k_head, step * block, block, 0)
                v_block = lax.dynamic_slice_in_dim(v_head, step * block, block, 0)
                k_pos = step * block + jnp.arange(block, dtype=jnp.int32)
                scores = jnp.dot(q_block, k_block.T, preferred_element_type=jnp.float32) * scale
                mask = k_pos[None, :] <= q_pos[:, None]
                new_max = jnp.maximum(run_max, lax.optimization_barrier(jnp.max(jnp.where(mask, scores, -1e+30), axis=1)))
                weights = jnp.where(mask, jnp.exp(scores - new_max[:, None]), 0.0)
                factor = jnp.exp(run_max - new_max)
                run_sum = run_sum * factor + lax.optimization_barrier(jnp.sum(weights, axis=1))
                accum = accum * factor[:, None] + jnp.dot(weights.astype(jnp.bfloat16), v_block, preferred_element_type=jnp.float32)
                return (new_max, run_sum, accum)
            start = (jnp.full((block,), -1e+30, jnp.float32), jnp.zeros((block,), jnp.float32), jnp.zeros((block, HD), jnp.float32))
            run_max, run_sum, accum = lax.fori_loop(0, index + 1, absorb, start)
            return (accum / run_sum[:, None]).astype(jnp.bfloat16)
        blocks = lax.map(one_block, jnp.arange(count, dtype=jnp.int32))
        return blocks.reshape(TOKENS, HD)
    heads_out = lax.map(one_head, (q_heads, k_heads, v_heads))
    attended = heads_out.transpose(1, 0, 2).reshape(TOKENS, D)
    return (attended, key_cache)
```

```python
import functools
import math

import jax
import jax.numpy as jnp
from jax import lax
from jax.experimental import pallas as pl
from jax.experimental.pallas import tpu as pltpu
from jax.sharding import Mesh, PartitionSpec as P

HD = 128
SCALE = 1.0 / math.sqrt(HD)
NZ, NX, NY, NC = 8, 4, 4, 2
T = 64
TOKENS = NZ * NX * NY * NC * T
SRC = NZ * NY
ROWS = SRC * T
TAIL = 16
G = NY * T
LOW, HIGH = 1e-25, 1e25
ALL = ("z", "x", "y", "core")
VMEM = pl.BlockSpec(memory_space=pltpu.VMEM)
ANY = pl.BlockSpec(memory_space=pl.ANY)


def dot_t(a, b):
    return lax.dot_general(a, b, (((1,), (1,)), ((), ())), preferred_element_type=jnp.float32)


def key_mean(sums_ref):
    return jnp.sum(sums_ref[...], axis=0, keepdims=True) / TOKENS


def column(z, x):
    return jnp.where(z % 2 == 0, x, NX - 1 - x)


def thirds(value):
    high = value.astype(jnp.bfloat16).astype(jnp.float32)
    mid = (value - high).astype(jnp.bfloat16).astype(jnp.float32)
    return high, mid, value - high - mid


def tail_rows(value, rows):
    which = lax.broadcasted_iota(jnp.int32, (rows, value.shape[1]), 0)
    high, mid, low = (jnp.broadcast_to(v, which.shape) for v in thirds(value))
    picked = jnp.where(which == 1, mid, jnp.where(which == 2, low, 0.0))
    return jnp.where(which == 0, high, picked).astype(jnp.bfloat16)


def copies(z, srcs, kc, vc, sems):
    out = []
    for s, halves in enumerate(srcs):
        n = NZ // len(halves)
        part = halves[z // n].at[pl.ds(z % n * NY, NY)]
        out.append(pltpu.make_async_copy(part.at[:, 0], kc.at[z, s], sems.at[z]))
        out.append(pltpu.make_async_copy(part.at[:, 1], vc.at[z, s], sems.at[z]))
    return out


def fetch(srcs, kc, vc, sems):
    for z in range(NZ):
        for copy in copies(z, srcs, kc, vc, sems):
            copy.start()


def ready(groups, mean, srcs, kc, vc, sems):
    for z in groups:
        for copy in copies(z, srcs, kc, vc, sems):
            copy.wait()

    @pl.loop(groups[0], groups[-1] + 1)
    def _(z):
        kc[z] = (kc[z].astype(jnp.float32) - mean).astype(jnp.bfloat16)


def attend(q, kc, vc, acc, tot, z, nz, kz, nk, first=0, count=None, mask=None):
    count = kc.shape[1] if count is None else count
    keys = nk * count * G
    at = pl.ds(pl.multiple_of(z * G, G), nz * G)
    ks = (pl.ds(kz, nk), pl.ds(first, count))
    p = jnp.exp(dot_t(q[at], kc[ks].reshape(keys, HD)) * SCALE)
    if mask is not None:
        p = jnp.where(mask, p, 0.0)
    part = p[:, :HD]
    for i in range(1, keys // HD):
        part = part + p[:, i * HD : (i + 1) * HD]
    tot[at] += part
    acc[at] += jnp.dot(
        p.astype(jnp.bfloat16), vc[ks].reshape(keys, HD), preferred_element_type=jnp.float32
    )


def work(mean, srcs, others, sems, q, kc, vc, acc, tot, mask=None):
    ns = len(srcs)
    refs = (q, kc, vc, acc, tot)
    ready(range(NZ // 2), mean, srcs, kc, vc, sems)
    nk = 8 // ns

    @pl.loop(0, 2 * (4 // nk))
    def _(i):
        attend(*refs, 4 + i % 2 * 2, 2, i // 2 * nk, nk)

    ready(range(NZ // 2, NZ), mean, srcs, kc, vc, sems)

    @pl.loop(0, 2)
    def _(i):
        attend(*refs, i * 4 + 2, 2, i * 4, 2)

    @pl.loop(0, 2)
    def _(i):
        for j in range(2):
            z = 4 * i + 2 * j
            attend(*refs, z + 1, 1, z, 1)

    if mask is not None:

        @pl.loop(0, 2)
        def _(i):
            for j in range(4):
                z = 4 * i + j
                attend(*refs, z, 1, z, 1, 0, 2, mask)

    z, x = lax.axis_index("z"), lax.axis_index("x")
    for first, shift in others:
        later = column(z, (x + shift) % NX) > column(z, x)
        odd = later.astype(jnp.int32)

        @pl.loop(0, 1)
        def _(i):
            for j in range(4):
                at = 4 * i + 2 * j + odd
                attend(*refs, at, 1, at, 1, first, 2)


def first_kernel(sums, q, o0, o1, l0, l1, acc, tot, kc, vc, sems):
    core = lax.axis_index("core")
    srcs = ([o0], [o1], [l0], [l1])
    fetch(srcs, kc, vc, sems)
    acc[...] = jnp.zeros_like(acc)
    tot[...] = jnp.zeros_like(tot)
    shape = (G, 2 * G)
    col = lax.broadcasted_iota(jnp.int32, shape, 1)
    kpos = (col % G) // T * (NC * T) + (core + col // G) % NC * T + col % T
    row = lax.broadcasted_iota(jnp.int32, shape, 0)
    qpos = row // T * (NC * T) + core * T + row % T
    work(key_mean(sums), srcs, [(2, NX - 1)], sems, q, kc, vc, acc, tot, kpos <= qpos)


def second_kernel(sums, q, r0, r1, acc_in, tot_in, acc, tot, kc, vc, sems, acc0, tot0, sem):
    srcs = ([r0], [r1])
    fetch(srcs, kc, vc, sems)
    state = state_in(acc_in, tot_in, acc0, tot0, sem)
    acc[...] = jnp.zeros_like(acc)
    tot[...] = jnp.zeros_like(tot)
    work(key_mean(sums), srcs, [(0, 1)], sems, q, kc, vc, acc, tot)
    for copy in state:
        copy.wait()
    acc[...] += acc0[...]
    tot[...] += tot0[...]


def state_in(acc_in, tot_in, acc0, tot0, sem):
    pair = [
        pltpu.make_async_copy(acc_in, acc0, sem.at[0]),
        pltpu.make_async_copy(tot_in, tot0, sem.at[1]),
    ]
    for copy in pair:
        copy.start()
    return pair


def robust(sums, q, srcs, out, acc, run_max, run_sum, stage):
    dz, x, core = lax.axis_index("z"), lax.axis_index("x"), lax.axis_index("core")
    mean = key_mean(sums)
    acc[...] = jnp.zeros_like(acc)
    run_sum[...] = jnp.zeros_like(run_sum)
    run_max[...] = jnp.full_like(run_max, -1e30)
    for s, halves in enumerate(srcs):
        kx = column(dz, (x + (0, NX - 1, 1, 2)[s // 2]) % NX)
        kcore = (core + s % 2) % NC
        n = SRC // len(halves)
        for h, src in enumerate(halves):
            pltpu.sync_copy(src, stage.at[pl.ds(h * n, n)])

        def block(i, carry):
            z, kz = i // NZ, i % NZ

            @pl.when(kz <= z)
            def _():
                at = pl.ds(pl.multiple_of(z * G, G), G)
                part = stage[pl.ds(kz * NY, NY)]
                k = (part[:, 0].reshape(G, HD).astype(jnp.float32) - mean).astype(jnp.bfloat16)
                scores = dot_t(q[at], k) * SCALE
                row = lax.broadcasted_iota(jnp.int32, (G, G), 0)
                col = lax.broadcasted_iota(jnp.int32, (G, G), 1)
                qpos = ((z * NX + column(z, column(dz, x))) * NY + row // T) * NC * T + core * T + row % T
                kpos = ((kz * NX + column(kz, kx)) * NY + col // T) * NC * T + kcore * T + col % T
                mask = kpos <= qpos
                old = run_max[at]
                new = jnp.maximum(
                    old, jnp.max(jnp.where(mask, scores, -1e30), axis=1, keepdims=True)
                )
                w = jnp.where(mask, jnp.exp(scores - new[:, :1]), 0.0)
                factor = jnp.exp(old - new)
                run_sum[at] = run_sum[at] * factor + jnp.sum(w, axis=1, keepdims=True)
                acc[at] = acc[at] * factor + jnp.dot(
                    w.astype(jnp.bfloat16),
                    part[:, 1].reshape(G, HD),
                    preferred_element_type=jnp.float32,
                )
                run_max[at] = new

            return carry

        lax.fori_loop(0, NZ * NZ, block, 0)
    out[:, :T] = (acc[...] / run_sum[...]).astype(jnp.bfloat16).reshape(SRC, T, HD)


def far_kernel(
    sums, q, a0, b0, a1, b1, acc_in, tot_in, o0, o1, l0, l1, r0, r1,
    out, acc, tot, kc, vc, sems, acc0, tot0, sem, stage,
):
    far = ([a0, b0], [a1, b1])
    fetch(far, kc, vc, sems)
    state = state_in(acc_in, tot_in, acc0, tot0, sem)
    acc[...] = jnp.zeros_like(acc)
    tot[...] = jnp.zeros_like(tot)
    work(key_mean(sums), far, [(0, 2)], sems, q, kc, vc, acc, tot)
    for copy in state:
        copy.wait()
    acc[...] += acc0[...]
    tot[...] += tot0[...]
    total = jnp.sum(tot[...], axis=1, keepdims=True)
    out[:, :T] = (acc[...] / total).astype(jnp.bfloat16).reshape(SRC, T, HD)
    tail = tail_rows(key_mean(sums), TAIL)
    out[:, T:] = jnp.broadcast_to(tail[None], (SRC, TAIL, HD))
    fine = jnp.where((total > LOW) & (total < HIGH), 0.0, 1.0)

    @pl.when(jnp.max(fine) > 0.0)
    def _():
        robust(sums, q, ([o0], [o1], [l0], [l1], [r0], [r1], *far), out, acc, acc0, tot, stage)


STATE = jax.ShapeDtypeStruct((ROWS, HD), jnp.float32)


def call(kernel, name, ins, outs, scratch, units):
    return functools.partial(
        pl.pallas_call(
            kernel,
            name=name,
            in_specs=ins,
            out_specs=[VMEM] * len(outs),
            out_shape=outs,
            scratch_shapes=scratch,
            compiler_params=pltpu.CompilerParams(vmem_limit_bytes=48 << 20),
            cost_estimate=pl.CostEstimate(
                flops=units * 32 * G * 2 * G * HD, bytes_accessed=4 << 20, transcendentals=0
            ),
        )
    )


def shards(queries, keys, values):
    def by_head(a):
        return a.reshape(T, SRC, HD).transpose(1, 0, 2)

    groups = [
        [
            ((z * NX + (x if z % 2 == 0 else NX - 1 - x)) * NY + y) * NC + core
            for z in range(NZ)
            for y in range(NY)
        ]
        for x in range(NX)
        for core in range(NC)
    ]

    def exchange(a):
        return lax.all_to_all(a, ALL, 0, 0, axis_index_groups=groups, tiled=True)

    kv = jnp.stack([by_head(keys), by_head(values)], axis=1)
    with jax.named_scope("kv_to_heads"):
        own = exchange(kv)
    queries, _ = lax.optimization_barrier((by_head(queries), own))
    with jax.named_scope("q_to_heads"):
        q = exchange(queries).reshape(ROWS, HD)
    right = [(i, (i + 1) % NX) for i in range(NX)]
    left = [(i, (i - 1) % NX) for i in range(NX)]
    across = [(i, (i + 2) % NX) for i in range(NX)]
    swap = [(0, 1), (1, 0)]
    half = SRC // 2
    with jax.named_scope("key_sums"):
        sums = jnp.sum(own[:, 0].astype(jnp.float32), axis=(0, 1))[None]
        sums = sums + lax.ppermute(sums, "core", swap)
        sums = jnp.concatenate([sums] + [lax.ppermute(sums, "x", p) for p in (right, left, across)])
    with jax.named_scope("ring"):
        l0 = lax.ppermute(own, "x", right)
        r0 = lax.ppermute(own, "x", left)
        o1 = lax.ppermute(own, "core", swap)
        l0, r0, q, sums = lax.optimization_barrier((l0, r0, q, sums))
        l1 = lax.ppermute(l0, "core", swap)
        r1 = lax.ppermute(r0, "core", swap)
        a0 = lax.ppermute(l0[:half], "x", right)
        b0 = lax.ppermute(r0[half:], "x", left)

    def bufs(ns):
        return [pltpu.VMEM((NZ, ns, NY, T, HD), jnp.bfloat16)] * 2 + [
            pltpu.SemaphoreType.DMA((NZ,))
        ]

    state = [pltpu.VMEM((ROWS, HD), jnp.float32)] * 2
    first = [VMEM] * 2 + [ANY] * 4
    acc, tot = call(first_kernel, "first", first, [STATE] * 2, bufs(4), 76)(sums, q, own, o1, l0, l1)
    a0, b0, acc, tot = lax.optimization_barrier((a0, b0, acc, tot))
    with jax.named_scope("ring"):
        a1 = lax.ppermute(a0, "core", swap)
        b1 = lax.ppermute(b0, "core", swap)
    acc, tot = call(
        second_kernel,
        "second",
        first,
        [STATE] * 2,
        bufs(2) + state + [pltpu.SemaphoreType.DMA((2,))],
        32,
    )(sums, q, r0, r1, acc, tot)
    (out,) = call(
        far_kernel,
        "far",
        [VMEM] * 2 + [ANY] * 12,
        [jax.ShapeDtypeStruct((SRC, T + TAIL, HD), jnp.bfloat16)],
        state
        + bufs(2)
        + state
        + [pltpu.SemaphoreType.DMA((2,)), pltpu.VMEM((SRC, 2, T, HD), jnp.bfloat16)],
        32,
    )(sums, q, a0, b0, a1, b1, acc, tot, own, o1, l0, l1, r0, r1)
    with jax.named_scope("home"):
        home = exchange(out)
    attended = home[:, :T].transpose(1, 0, 2).reshape(T, SRC * HD)
    parts = home[:, T : T + 3].astype(jnp.float32)
    mean = (parts[:, 0] + parts[:, 1] + parts[:, 2]).reshape(SRC * HD)
    key_cache = (keys.astype(jnp.float32) - mean).astype(jnp.bfloat16)
    return attended, key_cache


def solution(mesh):
    split = Mesh(mesh.devices.reshape(NZ, NX, NY, NC), ALL)
    spec = P(ALL, None)
    return jax.shard_map(
        shards, mesh=split, in_specs=(spec,) * 3, out_specs=(spec,) * 2, check_vma=False
    )
```

```python
import functools
import math

import jax
import jax.numpy as jnp
from jax import lax
from jax.experimental import pallas as pl
from jax.experimental.pallas import tpu as pltpu
from jax.sharding import Mesh, PartitionSpec as P

HD = 128
SCALE = 1.0 / math.sqrt(HD)
LOG2E = math.log2(math.e)
STEP = 512
VMEM_BYTES = 28 << 20
NZ, NX, NY, NC = 8, 4, 4, 2
T = 64
TOKENS = NZ * NX * NY * NC * T
SRC = NZ * NY
ROWS = SRC * T
TAIL = 16
G = NY * T
LOW, HIGH = 1e-25, 1e25
ALL = ("z", "x", "y", "core")
VMEM = pl.BlockSpec(memory_space=pltpu.VMEM)
ANY = pl.BlockSpec(memory_space=pl.ANY)


def dot_t(a, b):
    return lax.dot_general(a, b, (((1,), (1,)), ((), ())), preferred_element_type=jnp.float32)


def key_mean(q_ref):
    parts = q_ref[:, pl.ds(T, TAIL)].astype(jnp.float32)
    return jnp.sum(jnp.sum(parts, axis=0), axis=0, keepdims=True) / TOKENS


def thirds(value):
    high = value.astype(jnp.bfloat16).astype(jnp.float32)
    mid = (value - high).astype(jnp.bfloat16).astype(jnp.float32)
    return high, mid, value - high - mid


def tail_rows(value, rows):
    which = lax.broadcasted_iota(jnp.int32, (rows, value.shape[1]), 0)
    high, mid, low = (jnp.broadcast_to(v, which.shape) for v in thirds(value))
    picked = jnp.where(which == 1, mid, jnp.where(which == 2, low, 0.0))
    return jnp.where(which == 0, high, picked).astype(jnp.bfloat16)


def side(core):
    return NX - 1 + core * (2 - NX)


def copies(z, srcs, kc, vc, sems):
    out = []
    for s, src in enumerate(srcs):
        part = src.at[pl.ds(z * NY, NY)]
        out.append(pltpu.make_async_copy(part.at[:, 0], kc.at[z, s], sems.at[z]))
        out.append(pltpu.make_async_copy(part.at[:, 1], vc.at[z, s], sems.at[z]))
    return out


def fetch(srcs, kc, vc, sems):
    for z in range(NZ):
        for copy in copies(z, srcs, kc, vc, sems):
            copy.start()


def ready(groups, mean, srcs, kc, vc, sems):
    for z in groups:
        for copy in copies(z, srcs, kc, vc, sems):
            copy.wait()

    @pl.loop(groups[0], groups[-1] + 1)
    def _(z):
        kc[z] = (kc[z].astype(jnp.float32) - mean).astype(jnp.bfloat16)


def attend(q, kc, vc, acc, tot, z, nz, kz, nk, count=None, mask=None):
    count = kc.shape[1] if count is None else count
    keys = nk * count * G
    at = pl.ds(pl.multiple_of(z * G, G), nz * G)
    ks = (pl.ds(kz, nk), pl.ds(0, count))
    rows = q[pl.ds(z * NY, nz * NY), :T].reshape(nz * G, HD)
    k, v = kc[ks].reshape(keys, HD), vc[ks].reshape(keys, HD)
    part, added = None, None
    for i in range(0, keys, STEP):
        p = jnp.exp2(dot_t(rows, k[i : i + STEP]) * (SCALE * LOG2E))
        if mask is not None and i == 0:
            p = jnp.where(mask, p, 0.0)
        for j in range(0, STEP, HD):
            part = p[:, j : j + HD] if part is None else part + p[:, j : j + HD]
        o = jnp.dot(p.astype(jnp.bfloat16), v[i : i + STEP], preferred_element_type=jnp.float32)
        added = o if added is None else added + o
    tot[at] += part
    acc[at] += added


def work(mean, srcs, shift, sems, q, kc, vc, acc, tot, mask=None):
    ns = len(srcs)
    refs = (q, kc, vc, acc, tot)
    ready(range(NZ // 2), mean, srcs, kc, vc, sems)
    big = ns == 4

    @pl.loop(0, 2)
    def _(i):
        if big:
            attend(*refs, 4, 4, i * 2, 2)
        else:
            attend(*refs, 4 + i * 2, 2, 0, 4)

    ready(range(NZ // 2, NZ), mean, srcs, kc, vc, sems)

    @pl.loop(0, 2)
    def _(i):
        attend(*refs, i * 4 + 2, 2, i * 4, 2)

    x = lax.axis_index("x")
    earlier = (x + shift) % NX < x

    @pl.when(earlier)
    def _():
        @pl.loop(0, 2)
        def _(i):
            for j in range(2):
                z = 4 * i + 2 * j
                if mask is None:
                    attend(*refs, z, 2, z, 1)
                else:
                    attend(*refs, z + 1, 1, z, 1)
                    attend(*refs, z, 1, z, 1, ns, mask)
                attend(*refs, z + 1, 1, z + 1, 1, ns, mask)

    @pl.when(jnp.logical_not(earlier))
    def _():
        @pl.loop(0, 2)
        def _(i):
            for j in range(2):
                z = 4 * i + 2 * j
                attend(*refs, z + 1, 1, z, 1)
                if mask is not None:
                    attend(*refs, z, 1, z, 1, 2, mask)
                    attend(*refs, z + 1, 1, z + 1, 1, 2, mask)


def first_kernel(q, o0, o1, m0, m1, acc, tot, kc, vc, sems):
    core = lax.axis_index("core")
    srcs = (o0, o1, m0, m1)
    fetch(srcs, kc, vc, sems)
    acc[...] = jnp.zeros_like(acc)
    tot[...] = jnp.zeros_like(tot)
    shape = (G, 2 * G)
    col = lax.broadcasted_iota(jnp.int32, shape, 1)
    kpos = (col % G) // T * (NC * T) + (core + col // G) % NC * T + col % T
    row = lax.broadcasted_iota(jnp.int32, shape, 0)
    qpos = row // T * (NC * T) + core * T + row % T
    work(key_mean(q), srcs, side(core), sems, q, kc, vc, acc, tot, kpos <= qpos)


def second_kernel(q, s0, s1, acc_in, tot_in, acc, tot, kc, vc, sems, acc0, tot0, sem):
    core = lax.axis_index("core")
    srcs = (s0, s1)
    fetch(srcs, kc, vc, sems)
    state = state_in(acc_in, tot_in, acc0, tot0, sem)
    acc[...] = jnp.zeros_like(acc)
    tot[...] = jnp.zeros_like(tot)
    work(key_mean(q), srcs, side(1 - core), sems, q, kc, vc, acc, tot)
    for copy in state:
        copy.wait()
    acc[...] += acc0[...]
    tot[...] += tot0[...]


def state_in(acc_in, tot_in, acc0, tot0, sem):
    pair = [
        pltpu.make_async_copy(acc_in, acc0, sem.at[0]),
        pltpu.make_async_copy(tot_in, tot0, sem.at[1]),
    ]
    for copy in pair:
        copy.start()
    return pair


def robust(q, srcs, out, acc, run_max, run_sum, stage):
    x, core = lax.axis_index("x"), lax.axis_index("core")
    mean = key_mean(q)
    acc[...] = jnp.zeros_like(acc)
    run_sum[...] = jnp.zeros_like(run_sum)
    run_max[...] = jnp.full_like(run_max, -1e30)
    for s, src in enumerate(srcs):
        kx = (x + (0, side(core), side(1 - core), 2)[s // 2]) % NX
        kcore = (core + s % 2) % NC
        pltpu.sync_copy(src, stage)

        def block(i, carry):
            z, kz = i // NZ, i % NZ

            @pl.when(kz <= z)
            def _():
                at = pl.ds(pl.multiple_of(z * G, G), G)
                part = stage[pl.ds(kz * NY, NY)]
                k = (part[:, 0].reshape(G, HD).astype(jnp.float32) - mean).astype(jnp.bfloat16)
                scores = dot_t(q[pl.ds(z * NY, NY), :T].reshape(G, HD), k) * SCALE
                row = lax.broadcasted_iota(jnp.int32, (G, G), 0)
                col = lax.broadcasted_iota(jnp.int32, (G, G), 1)
                qpos = ((z * NX + x) * NY + row // T) * NC * T + core * T + row % T
                kpos = ((kz * NX + kx) * NY + col // T) * NC * T + kcore * T + col % T
                mask = kpos <= qpos
                old = run_max[at]
                new = jnp.maximum(
                    old, jnp.max(jnp.where(mask, scores, -1e30), axis=1, keepdims=True)
                )
                w = jnp.where(mask, jnp.exp(scores - new[:, :1]), 0.0)
                factor = jnp.exp(old - new)
                run_sum[at] = run_sum[at] * factor + jnp.sum(w, axis=1, keepdims=True)
                acc[at] = acc[at] * factor + jnp.dot(
                    w.astype(jnp.bfloat16),
                    part[:, 1].reshape(G, HD),
                    preferred_element_type=jnp.float32,
                )
                run_max[at] = new

            return carry

        lax.fori_loop(0, NZ * NZ, block, 0)
    out[:, :T] = (acc[...] / run_sum[...]).astype(jnp.bfloat16).reshape(SRC, T, HD)


def far_kernel(
    q, f0, f1, acc_in, tot_in, o0, o1, m0, m1, s0, s1,
    out, acc, tot, kc, vc, sems, acc0, tot0, sem, stage,
):
    far = (f0, f1)
    fetch(far, kc, vc, sems)
    state = state_in(acc_in, tot_in, acc0, tot0, sem)
    acc[...] = jnp.zeros_like(acc)
    tot[...] = jnp.zeros_like(tot)
    work(key_mean(q), far, 2, sems, q, kc, vc, acc, tot)
    for copy in state:
        copy.wait()
    acc[...] += acc0[...]
    tot[...] += tot0[...]
    total = jnp.sum(tot[...], axis=1, keepdims=True)
    out[:, :T] = (acc[...] / total).astype(jnp.bfloat16).reshape(SRC, T, HD)
    tail = tail_rows(key_mean(q), TAIL)
    out[:, T:] = jnp.broadcast_to(tail[None], (SRC, TAIL, HD))
    fine = jnp.where((total > LOW) & (total < HIGH), 0.0, 1.0)

    @pl.when(jnp.max(fine) > 0.0)
    def _():
        robust(q, (o0, o1, m0, m1, s0, s1, f0, f1), out, acc, acc0, tot, stage)


STATE = jax.ShapeDtypeStruct((ROWS, HD), jnp.float32)


def call(kernel, name, ins, outs, scratch, units):
    return functools.partial(
        pl.pallas_call(
            kernel,
            name=name,
            in_specs=ins,
            out_specs=[VMEM] * len(outs),
            out_shape=outs,
            scratch_shapes=scratch,
            compiler_params=pltpu.CompilerParams(vmem_limit_bytes=VMEM_BYTES),
            cost_estimate=pl.CostEstimate(
                flops=units * 32 * G * 2 * G * HD, bytes_accessed=4 << 20, transcendentals=0
            ),
        )
    )


def shards(queries, keys, values):
    def by_head(a):
        return a.reshape(T, SRC, HD).transpose(1, 0, 2)

    def exchange(a):
        return lax.all_to_all(a, ("z", "y"), 0, 0, tiled=True)

    right = [(i, (i + 1) % NX) for i in range(NX)]
    left = [(i, (i - 1) % NX) for i in range(NX)]
    across = [(i, (i + 2) % NX) for i in range(NX)]
    swap = [(0, 1), (1, 0)]
    kv = jnp.stack([by_head(keys), by_head(values)], axis=1)
    with jax.named_scope("kv_to_heads"):
        own = exchange(kv)
    with jax.named_scope("key_sums"):
        sums = jnp.sum(keys.astype(jnp.float32), axis=0).reshape(SRC, HD)
        sums = sums + lax.ppermute(sums, "core", swap)
        sums = sums + sum(lax.ppermute(sums, "x", p) for p in (right, left, across))
        high = lax.reduce_precision(sums, 8, 7)
        mid = lax.reduce_precision(sums - high, 8, 7)
        parts = jnp.stack([high, mid, sums - high - mid], axis=1).astype(jnp.bfloat16)
        parts = jnp.pad(parts, ((0, 0), (0, TAIL - 3), (0, 0)))
    queries, parts, own = lax.optimization_barrier((queries, parts, own))
    with jax.named_scope("q_to_heads"):
        q = exchange(jnp.concatenate([by_head(queries), parts], axis=1))
    ring = [(NC * i, NC * j) for i, j in right] + [(NC * i + 1, NC * j + 1) for i, j in left]
    with jax.named_scope("ring"):
        m0 = lax.ppermute(own, ("x", "core"), ring)
        o1 = lax.ppermute(own, "core", swap)
        m1 = lax.ppermute(o1, ("x", "core"), ring)
        s1 = lax.ppermute(m0, "core", swap)
        s1, q = lax.optimization_barrier((s1, q))
        m0, m1 = lax.optimization_barrier((m0, m1))
        f0 = lax.ppermute(m0, ("x", "core"), ring)
        s0 = lax.ppermute(m1, "core", swap)

    def bufs(ns):
        return [pltpu.VMEM((NZ, ns, NY, T, HD), jnp.bfloat16)] * 2 + [
            pltpu.SemaphoreType.DMA((NZ,))
        ]

    state = [pltpu.VMEM((ROWS, HD), jnp.float32)] * 2
    first = [VMEM] + [ANY] * 4
    acc, tot = call(first_kernel, "first", first, [STATE] * 2, bufs(4), 76)(q, own, o1, m0, m1)
    f0, acc, tot = lax.optimization_barrier((f0, acc, tot))
    with jax.named_scope("ring"):
        f1 = lax.ppermute(f0, "core", swap)
    acc, tot = call(
        second_kernel,
        "second",
        first,
        [STATE] * 2,
        bufs(2) + state + [pltpu.SemaphoreType.DMA((2,))],
        32,
    )(q, s0, s1, acc, tot)
    (out,) = call(
        far_kernel,
        "far",
        [VMEM] + [ANY] * 10,
        [jax.ShapeDtypeStruct((SRC, T + TAIL, HD), jnp.bfloat16)],
        state
        + bufs(2)
        + state
        + [pltpu.SemaphoreType.DMA((2,)), pltpu.VMEM((SRC, 2, T, HD), jnp.bfloat16)],
        32,
    )(q, f0, f1, acc, tot, own, o1, m0, m1, s0, s1)
    with jax.named_scope("home"):
        home = exchange(out)
    attended = home[:, :T].transpose(1, 0, 2).reshape(T, SRC * HD)
    parts = home[:, T : T + 3].astype(jnp.float32)
    mean = (parts[:, 0] + parts[:, 1] + parts[:, 2]).reshape(SRC * HD)
    key_cache = (keys.astype(jnp.float32) - mean).astype(jnp.bfloat16)
    return attended, key_cache


def solution(mesh):
    split = Mesh(mesh.devices.reshape(NZ, NX, NY, NC), ALL)
    spec = P(ALL, None)
    return jax.shard_map(
        shards, mesh=split, in_specs=(spec,) * 3, out_specs=(spec,) * 2, check_vma=False
    )
```

```python
import functools
import math

import jax
import jax.numpy as jnp
from jax import lax
from jax.experimental import pallas as pl
from jax.experimental.pallas import tpu as pltpu
from jax.sharding import Mesh, PartitionSpec as P

HD = 128
SCALE = 1.0 / math.sqrt(HD)
LOG2E = math.log2(math.e)
STEP = 512
VMEM_BYTES = 20 << 20
NZ, NX, NY, NC = 8, 4, 4, 2
T = 64
TOKENS = NZ * NX * NY * NC * T
SRC = NZ * NY
ROWS = SRC * T
TAIL = 16
G = NY * T
LOW, HIGH = 1e-25, 1e25
ALL = ("z", "x", "y", "core")
VMEM = pl.BlockSpec(memory_space=pltpu.VMEM)
ANY = pl.BlockSpec(memory_space=pl.ANY)


def dot_t(a, b):
    return lax.dot_general(a, b, (((1,), (1,)), ((), ())), preferred_element_type=jnp.float32)


def key_mean(q_ref):
    parts = q_ref[:, pl.ds(T, TAIL)].astype(jnp.float32)
    return jnp.sum(jnp.sum(parts, axis=0), axis=0, keepdims=True) / TOKENS


def thirds(value):
    high = value.astype(jnp.bfloat16).astype(jnp.float32)
    mid = (value - high).astype(jnp.bfloat16).astype(jnp.float32)
    return high, mid, value - high - mid


def tail_rows(value, rows):
    which = lax.broadcasted_iota(jnp.int32, (rows, value.shape[1]), 0)
    high, mid, low = (jnp.broadcast_to(v, which.shape) for v in thirds(value))
    picked = jnp.where(which == 1, mid, jnp.where(which == 2, low, 0.0))
    return jnp.where(which == 0, high, picked).astype(jnp.bfloat16)


def side(core):
    return NX - 1 + core * (2 - NX)


def copies(z, srcs, kc, vc, sems):
    out = []
    for s, src in enumerate(srcs):
        part = src.at[pl.ds(z * NY, NY)]
        out.append(pltpu.make_async_copy(part.at[:, 0], kc.at[z, s], sems.at[z]))
        out.append(pltpu.make_async_copy(part.at[:, 1], vc.at[z, s], sems.at[z]))
    return out


def fetch(srcs, kc, vc, sems):
    for z in range(NZ):
        for copy in copies(z, srcs, kc, vc, sems):
            copy.start()


def ready(first, count, mean, srcs, kc, vc, sems):
    for i in range(count):
        for copy in copies(first + i, srcs, kc, vc, sems):
            copy.wait()
        kc[first + i] = (kc[first + i].astype(jnp.float32) - mean).astype(jnp.bfloat16)


def attend(q, kc, vc, acc, tot, z, nz, kz, nk, count=None, masks=None):
    count = kc.shape[1] if count is None else count
    keys = nk * count * G
    at = pl.ds(pl.multiple_of(z * G, G), nz * G)
    ks = (pl.ds(kz, nk), pl.ds(0, count))
    rows = q[pl.ds(z * NY, nz * NY), :T].reshape(nz * G, HD)
    k, v = kc[ks].reshape(keys, HD), vc[ks].reshape(keys, HD)
    part, added = None, None
    for i in range(0, keys, STEP):
        p = jnp.exp2(dot_t(rows, k[i : i + STEP]) * (SCALE * LOG2E))
        if masks is not None:
            p = jnp.where(masks[i // STEP], p, 0.0)
        for j in range(0, STEP, HD):
            part = p[:, j : j + HD] if part is None else part + p[:, j : j + HD]
        o = jnp.dot(p.astype(jnp.bfloat16), v[i : i + STEP], preferred_element_type=jnp.float32)
        added = o if added is None else added + o
    tot[at] += part
    acc[at] += added


def work(mean, srcs, shifts, sems, q, kc, vc, acc, tot, own=None):
    ns = len(srcs)
    refs = (q, kc, vc, acc, tot)

    @pl.loop(0, 2)
    def _(i):
        ready(i * 2, 2, mean, srcs, kc, vc, sems)
        attend(*refs, 4, 4, i * 2, 2)

    ready(4, 4, mean, srcs, kc, vc, sems)

    @pl.loop(0, 2)
    def _(i):
        attend(*refs, i * 4 + 2, 2, i * 4, 2)

    x = lax.axis_index("x")
    first, second = ((x + shift) % NX < x for shift in shifts)
    some = jnp.logical_or(first, second)

    def allowed(rows):
        at = lax.broadcasted_iota(jnp.int32, (rows, 2 * G), 1)
        ok = jnp.where(at < G, first.astype(jnp.int32), second.astype(jnp.int32))
        if rows > G:
            ok = jnp.where(lax.broadcasted_iota(jnp.int32, ok.shape, 0) < G, ok, 1)
        return ok > 0

    @pl.when(some)
    def _():
        @pl.loop(0, 2)
        def _(i):
            one = allowed(G)
            masks = [one] if own is None else [own, one]
            for j in range(2):
                z = 4 * i + 2 * j
                if own is None:
                    attend(*refs, z, 2, z, 1, ns, [allowed(2 * G)])
                else:
                    attend(*refs, z + 1, 1, z, 1)
                    attend(*refs, z, 1, z, 1, ns, masks)
                attend(*refs, z + 1, 1, z + 1, 1, ns, masks)

    @pl.when(jnp.logical_not(some))
    def _():
        @pl.loop(0, 2)
        def _(i):
            for j in range(2):
                z = 4 * i + 2 * j
                attend(*refs, z + 1, 1, z, 1)
                if own is not None:
                    attend(*refs, z, 1, z, 1, 2, [own])
                    attend(*refs, z + 1, 1, z + 1, 1, 2, [own])


def first_kernel(q, o0, o1, m0, s1, acc, tot, kc, vc, sems):
    core = lax.axis_index("core")
    srcs = (o0, o1, m0, s1)
    fetch(srcs, kc, vc, sems)
    acc[...] = jnp.zeros_like(acc)
    tot[...] = jnp.zeros_like(tot)
    shape = (G, 2 * G)
    col = lax.broadcasted_iota(jnp.int32, shape, 1)
    kpos = (col % G) // T * (NC * T) + (core + col // G) % NC * T + col % T
    row = lax.broadcasted_iota(jnp.int32, shape, 0)
    qpos = row // T * (NC * T) + core * T + row % T
    shifts = side(core), side(1 - core)
    work(key_mean(q), srcs, shifts, sems, q, kc, vc, acc, tot, kpos <= qpos)


def second_kernel(q, m1, f0, acc_in, tot_in, acc, tot, kc, vc, sems, acc0, tot0, sem):
    srcs = (m1, f0)
    fetch(srcs, kc, vc, sems)
    state = state_in(acc_in, tot_in, acc0, tot0, sem)
    acc[...] = jnp.zeros_like(acc)
    tot[...] = jnp.zeros_like(tot)
    shifts = side(lax.axis_index("core")), 2
    work(key_mean(q), srcs, shifts, sems, q, kc, vc, acc, tot)
    for copy in state:
        copy.wait()
    acc[...] += acc0[...]
    tot[...] += tot0[...]


def state_in(acc_in, tot_in, acc0, tot0, sem):
    pair = [
        pltpu.make_async_copy(acc_in, acc0, sem.at[0]),
        pltpu.make_async_copy(tot_in, tot0, sem.at[1]),
    ]
    for copy in pair:
        copy.start()
    return pair


def robust(q, srcs, out, acc, run_max, run_sum, stage):
    x, core = lax.axis_index("x"), lax.axis_index("core")
    mean = key_mean(q)
    acc[...] = jnp.zeros_like(acc)
    run_sum[...] = jnp.zeros_like(run_sum)
    run_max[...] = jnp.full_like(run_max, -1e30)
    for src, shift, other in srcs:
        kx = (x + shift) % NX
        kcore = (core + other) % NC
        pltpu.sync_copy(src, stage)

        def block(i, carry):
            z, kz = i // NZ, i % NZ

            @pl.when(kz <= z)
            def _():
                at = pl.ds(pl.multiple_of(z * G, G), G)
                part = stage[pl.ds(kz * NY, NY)]
                k = (part[:, 0].reshape(G, HD).astype(jnp.float32) - mean).astype(jnp.bfloat16)
                scores = dot_t(q[pl.ds(z * NY, NY), :T].reshape(G, HD), k) * SCALE
                row = lax.broadcasted_iota(jnp.int32, (G, G), 0)
                col = lax.broadcasted_iota(jnp.int32, (G, G), 1)
                qpos = ((z * NX + x) * NY + row // T) * NC * T + core * T + row % T
                kpos = ((kz * NX + kx) * NY + col // T) * NC * T + kcore * T + col % T
                mask = kpos <= qpos
                old = run_max[at]
                new = jnp.maximum(
                    old, jnp.max(jnp.where(mask, scores, -1e30), axis=1, keepdims=True)
                )
                w = jnp.where(mask, jnp.exp(scores - new[:, :1]), 0.0)
                factor = jnp.exp(old - new)
                run_sum[at] = run_sum[at] * factor + jnp.sum(w, axis=1, keepdims=True)
                acc[at] = acc[at] * factor + jnp.dot(
                    w.astype(jnp.bfloat16),
                    part[:, 1].reshape(G, HD),
                    preferred_element_type=jnp.float32,
                )
                run_max[at] = new

            return carry

        lax.fori_loop(0, NZ * NZ, block, 0)
    out[:, :T] = (acc[...] / run_sum[...]).astype(jnp.bfloat16).reshape(SRC, T, HD)


def third_kernel(
    q, s0, f1, acc_in, tot_in, o0, o1, m0, s1, m1, f0,
    out, acc, tot, kc, vc, sems, acc0, tot0, sem, stage,
):
    core = lax.axis_index("core")
    last = (s0, f1)
    fetch(last, kc, vc, sems)
    state = state_in(acc_in, tot_in, acc0, tot0, sem)
    acc[...] = jnp.zeros_like(acc)
    tot[...] = jnp.zeros_like(tot)
    work(key_mean(q), last, (side(1 - core), 2), sems, q, kc, vc, acc, tot)
    for copy in state:
        copy.wait()
    acc[...] += acc0[...]
    tot[...] += tot0[...]
    total = jnp.sum(tot[...], axis=1, keepdims=True)
    out[:, :T] = (acc[...] * (1.0 / total)).astype(jnp.bfloat16).reshape(SRC, T, HD)
    tail = tail_rows(key_mean(q), TAIL)
    out[:, T:] = jnp.broadcast_to(tail[None], (SRC, TAIL, HD))
    fine = jnp.where((total > LOW) & (total < HIGH), 0.0, 1.0)

    @pl.when(jnp.max(fine) > 0.0)
    def _():
        near, away = side(core), side(1 - core)
        srcs = [(o0, 0, 0), (o1, 0, 1), (m0, near, 0), (s1, away, 1)]
        srcs += [(m1, near, 1), (f0, 2, 0), (s0, away, 0), (f1, 2, 1)]
        robust(q, srcs, out, acc, acc0, tot, stage)


STATE = jax.ShapeDtypeStruct((ROWS, HD), jnp.float32)


def call(kernel, name, ins, outs, scratch, units):
    return functools.partial(
        pl.pallas_call(
            kernel,
            name=name,
            in_specs=ins,
            out_specs=[VMEM] * len(outs),
            out_shape=outs,
            scratch_shapes=scratch,
            compiler_params=pltpu.CompilerParams(vmem_limit_bytes=VMEM_BYTES),
            cost_estimate=pl.CostEstimate(
                flops=units * 32 * G * 2 * G * HD, bytes_accessed=4 << 20, transcendentals=0
            ),
        )
    )


def shards(queries, keys, values):
    def by_head(a):
        return a.reshape(T, SRC, HD).transpose(1, 0, 2)

    def exchange(a):
        return lax.all_to_all(a, ("z", "y"), 0, 0, tiled=True)

    right = [(i, (i + 1) % NX) for i in range(NX)]
    left = [(i, (i - 1) % NX) for i in range(NX)]
    across = [(i, (i + 2) % NX) for i in range(NX)]
    swap = [(0, 1), (1, 0)]
    kv = jnp.stack([by_head(keys), by_head(values)], axis=1)
    with jax.named_scope("kv_to_heads"):
        own = exchange(kv)
    with jax.named_scope("key_sums"):
        sums = jnp.sum(keys.astype(jnp.float32), axis=0).reshape(SRC, HD)
        sums = sums + lax.ppermute(sums, "core", swap)
        sums = sums + sum(lax.ppermute(sums, "x", p) for p in (right, left, across))
        high = lax.reduce_precision(sums, 8, 7)
        mid = lax.reduce_precision(sums - high, 8, 7)
        parts = jnp.stack([high, mid, sums - high - mid], axis=1).astype(jnp.bfloat16)
        parts = jnp.pad(parts, ((0, 0), (0, TAIL - 3), (0, 0)))
    queries, parts, own = lax.optimization_barrier((queries, parts, own))
    with jax.named_scope("q_to_heads"):
        q = exchange(jnp.concatenate([by_head(queries), parts], axis=1))
    ring = [(NC * i, NC * j) for i, j in right] + [(NC * i + 1, NC * j + 1) for i, j in left]
    with jax.named_scope("ring"):
        m0 = lax.ppermute(own, ("x", "core"), ring)
        o1 = lax.ppermute(own, "core", swap)
        m1 = lax.ppermute(o1, ("x", "core"), ring)
        s1 = lax.ppermute(m0, "core", swap)
        s1, q = lax.optimization_barrier((s1, q))
        f0 = lax.ppermute(m0, ("x", "core"), ring)

    def bufs(ns):
        return [pltpu.VMEM((NZ, ns, NY, T, HD), jnp.bfloat16)] * 2 + [
            pltpu.SemaphoreType.DMA((NZ,))
        ]

    state = [pltpu.VMEM((ROWS, HD), jnp.float32)] * 2
    first = [VMEM] + [ANY] * 4
    acc, tot = call(first_kernel, "first", first, [STATE] * 2, bufs(4), 76)(q, own, o1, m0, s1)
    m1, f0, acc, tot = lax.optimization_barrier((m1, f0, acc, tot))
    with jax.named_scope("ring"):
        s0 = lax.ppermute(m1, "core", swap)
        f1 = lax.ppermute(f0, "core", swap)
    acc, tot = call(
        second_kernel,
        "second",
        first,
        [STATE] * 2,
        bufs(2) + state + [pltpu.SemaphoreType.DMA((2,))],
        36,
    )(q, m1, f0, acc, tot)
    (out,) = call(
        third_kernel,
        "third",
        [VMEM] + [ANY] * 10,
        [jax.ShapeDtypeStruct((SRC, T + TAIL, HD), jnp.bfloat16)],
        state
        + bufs(2)
        + state
        + [pltpu.SemaphoreType.DMA((2,)), pltpu.VMEM((SRC, 2, T, HD), jnp.bfloat16)],
        36,
    )(q, s0, f1, acc, tot, own, o1, m0, s1, m1, f0)
    with jax.named_scope("home"):
        home = exchange(out)
    attended = home[:, :T].transpose(1, 0, 2).reshape(T, SRC * HD)
    parts = home[:, T : T + 3].astype(jnp.float32)
    mean = (parts[:, 0] + parts[:, 1] + parts[:, 2]).reshape(SRC * HD)
    key_cache = (keys.astype(jnp.float32) - mean).astype(jnp.bfloat16)
    return attended, key_cache


def solution(mesh):
    split = Mesh(mesh.devices.reshape(NZ, NX, NY, NC), ALL)
    spec = P(ALL, None)
    return jax.shard_map(
        shards, mesh=split, in_specs=(spec,) * 3, out_specs=(spec,) * 2, check_vma=False
    )
```

```python
import functools
import math

import jax
import jax.numpy as jnp
from jax import lax
from jax.experimental import pallas as pl
from jax.experimental.pallas import tpu as pltpu
from jax.sharding import Mesh, PartitionSpec as P

HD = 128
SCALE = 1.0 / math.sqrt(HD)
LOG2E = math.log2(math.e)
STEP = 1024
VMEM_BYTES = 20 << 20
NZ, NX, NY, NC = 8, 4, 4, 2
T = 64
TOKENS = NZ * NX * NY * NC * T
SRC = NZ * NY
ROWS = SRC * T
TAIL = 16
G = NY * T
LOW, HIGH = 1e-25, 1e25
ALL = ("z", "x", "y", "core")
VMEM = pl.BlockSpec(memory_space=pltpu.VMEM)
ANY = pl.BlockSpec(memory_space=pl.ANY)


def dot_t(a, b):
    return lax.dot_general(a, b, (((1,), (1,)), ((), ())), preferred_element_type=jnp.float32)


def key_mean(q_ref):
    parts = q_ref[:, pl.ds(T, TAIL)].astype(jnp.float32)
    return jnp.sum(jnp.sum(parts, axis=0), axis=0, keepdims=True) / TOKENS


def thirds(value):
    high = value.astype(jnp.bfloat16).astype(jnp.float32)
    mid = (value - high).astype(jnp.bfloat16).astype(jnp.float32)
    return high, mid, value - high - mid


def tail_rows(value, rows):
    which = lax.broadcasted_iota(jnp.int32, (rows, value.shape[1]), 0)
    high, mid, low = (jnp.broadcast_to(v, which.shape) for v in thirds(value))
    picked = jnp.where(which == 1, mid, jnp.where(which == 2, low, 0.0))
    return jnp.where(which == 0, high, picked).astype(jnp.bfloat16)


def side(core):
    return NX - 1 + core * (2 - NX)


def copies(z, srcs, kc, vc, sems):
    out = []
    for s, src in enumerate(srcs):
        part = src.at[pl.ds(z * NY, NY)]
        out.append(pltpu.make_async_copy(part.at[:, 0], kc.at[z, s], sems.at[z]))
        out.append(pltpu.make_async_copy(part.at[:, 1], vc.at[z, s], sems.at[z]))
    return out


def fetch(srcs, kc, vc, sems):
    for z in range(NZ):
        for copy in copies(z, srcs, kc, vc, sems):
            copy.start()


def ready(first, count, mean, srcs, kc, vc, sems):
    for i in range(count):
        for copy in copies(first + i, srcs, kc, vc, sems):
            copy.wait()
        kc[first + i] = (kc[first + i].astype(jnp.float32) - mean).astype(jnp.bfloat16)


def attend(q, kc, vc, acc, tot, z, nz, kz, nk, count=None, masks=None):
    count = kc.shape[1] if count is None else count
    keys = nk * count * G
    at = pl.ds(pl.multiple_of(z * G, G), nz * G)
    ks = (pl.ds(kz, nk), pl.ds(0, count))
    rows = q[pl.ds(z * NY, nz * NY), :T].reshape(nz * G, HD)
    k, v = kc[ks].reshape(keys, HD), vc[ks].reshape(keys, HD)
    part, added = None, None
    step = min(STEP if masks is None else STEP // 2, keys)
    for i in range(0, keys, step):
        p = jnp.exp2(dot_t(rows, k[i : i + step]) * (SCALE * LOG2E))
        if masks is not None:
            p = jnp.where(masks[i // step], p, 0.0)
        for j in range(0, step, HD):
            part = p[:, j : j + HD] if part is None else part + p[:, j : j + HD]
        o = jnp.dot(p.astype(jnp.bfloat16), v[i : i + step], preferred_element_type=jnp.float32)
        added = o if added is None else added + o
    tot[at] += part
    acc[at] += added


def work(mean, srcs, shifts, sems, q, kc, vc, acc, tot, own=None):
    ns = len(srcs)
    refs = (q, kc, vc, acc, tot)

    @pl.loop(0, 2)
    def _(i):
        ready(i * 2, 2, mean, srcs, kc, vc, sems)
        attend(*refs, 4, 4, i * 2, 2)

    ready(4, 4, mean, srcs, kc, vc, sems)

    @pl.loop(0, 2)
    def _(i):
        attend(*refs, i * 4 + 2, 2, i * 4, 2)

    x = lax.axis_index("x")
    first, second = ((x + shift) % NX < x for shift in shifts)
    some = jnp.logical_or(first, second)

    def allowed(rows):
        at = lax.broadcasted_iota(jnp.int32, (rows, 2 * G), 1)
        ok = jnp.where(at < G, first.astype(jnp.int32), second.astype(jnp.int32))
        if rows > G:
            ok = jnp.where(lax.broadcasted_iota(jnp.int32, ok.shape, 0) < G, ok, 1)
        return ok > 0

    @pl.when(some)
    def _():
        @pl.loop(0, 2)
        def _(i):
            one = allowed(G)
            masks = [one] if own is None else [own, one]
            for j in range(2):
                z = 4 * i + 2 * j
                if own is None:
                    attend(*refs, z, 2, z, 1, ns, [allowed(2 * G)])
                else:
                    attend(*refs, z + 1, 1, z, 1)
                    attend(*refs, z, 1, z, 1, ns, masks)
                attend(*refs, z + 1, 1, z + 1, 1, ns, masks)

    @pl.when(jnp.logical_not(some))
    def _():
        @pl.loop(0, 2)
        def _(i):
            for j in range(2):
                z = 4 * i + 2 * j
                attend(*refs, z + 1, 1, z, 1)
                if own is not None:
                    attend(*refs, z, 1, z, 1, 2, [own])
                    attend(*refs, z + 1, 1, z + 1, 1, 2, [own])


def first_kernel(q, o0, o1, m0, s1, acc, tot, kc, vc, sems):
    core = lax.axis_index("core")
    srcs = (o0, o1, m0, s1)
    fetch(srcs, kc, vc, sems)
    acc[...] = jnp.zeros_like(acc)
    tot[...] = jnp.zeros_like(tot)
    shape = (G, 2 * G)
    col = lax.broadcasted_iota(jnp.int32, shape, 1)
    kpos = (col % G) // T * (NC * T) + (core + col // G) % NC * T + col % T
    row = lax.broadcasted_iota(jnp.int32, shape, 0)
    qpos = row // T * (NC * T) + core * T + row % T
    shifts = side(core), side(1 - core)
    work(key_mean(q), srcs, shifts, sems, q, kc, vc, acc, tot, kpos <= qpos)


def second_kernel(q, m1, f0, acc_in, tot_in, acc, tot, kc, vc, sems, acc0, tot0, sem):
    srcs = (m1, f0)
    fetch(srcs, kc, vc, sems)
    state = state_in(acc_in, tot_in, acc0, tot0, sem)
    acc[...] = jnp.zeros_like(acc)
    tot[...] = jnp.zeros_like(tot)
    shifts = side(lax.axis_index("core")), 2
    work(key_mean(q), srcs, shifts, sems, q, kc, vc, acc, tot)
    for copy in state:
        copy.wait()
    acc[...] += acc0[...]
    tot[...] += tot0[...]


def state_in(acc_in, tot_in, acc0, tot0, sem):
    pair = [
        pltpu.make_async_copy(acc_in, acc0, sem.at[0]),
        pltpu.make_async_copy(tot_in, tot0, sem.at[1]),
    ]
    for copy in pair:
        copy.start()
    return pair


def robust(q, srcs, out, acc, run_max, run_sum, stage):
    x, core = lax.axis_index("x"), lax.axis_index("core")
    mean = key_mean(q)
    acc[...] = jnp.zeros_like(acc)
    run_sum[...] = jnp.zeros_like(run_sum)
    run_max[...] = jnp.full_like(run_max, -1e30)
    for src, shift, other in srcs:
        kx = (x + shift) % NX
        kcore = (core + other) % NC
        pltpu.sync_copy(src, stage)

        def block(i, carry):
            z, kz = i // NZ, i % NZ

            @pl.when(kz <= z)
            def _():
                at = pl.ds(pl.multiple_of(z * G, G), G)
                part = stage[pl.ds(kz * NY, NY)]
                k = (part[:, 0].reshape(G, HD).astype(jnp.float32) - mean).astype(jnp.bfloat16)
                scores = dot_t(q[pl.ds(z * NY, NY), :T].reshape(G, HD), k) * SCALE
                row = lax.broadcasted_iota(jnp.int32, (G, G), 0)
                col = lax.broadcasted_iota(jnp.int32, (G, G), 1)
                qpos = ((z * NX + x) * NY + row // T) * NC * T + core * T + row % T
                kpos = ((kz * NX + kx) * NY + col // T) * NC * T + kcore * T + col % T
                mask = kpos <= qpos
                old = run_max[at]
                new = jnp.maximum(
                    old, jnp.max(jnp.where(mask, scores, -1e30), axis=1, keepdims=True)
                )
                w = jnp.where(mask, jnp.exp(scores - new[:, :1]), 0.0)
                factor = jnp.exp(old - new)
                run_sum[at] = run_sum[at] * factor + jnp.sum(w, axis=1, keepdims=True)
                acc[at] = acc[at] * factor + jnp.dot(
                    w.astype(jnp.bfloat16),
                    part[:, 1].reshape(G, HD),
                    preferred_element_type=jnp.float32,
                )
                run_max[at] = new

            return carry

        lax.fori_loop(0, NZ * NZ, block, 0)
    out[:, :T] = (acc[...] / run_sum[...]).astype(jnp.bfloat16).reshape(SRC, T, HD)


def third_kernel(
    q, s0, f1, acc_in, tot_in, o0, o1, m0, s1, m1, f0,
    out, acc, tot, kc, vc, sems, acc0, tot0, sem, stage,
):
    core = lax.axis_index("core")
    last = (s0, f1)
    fetch(last, kc, vc, sems)
    state = state_in(acc_in, tot_in, acc0, tot0, sem)
    acc[...] = jnp.zeros_like(acc)
    tot[...] = jnp.zeros_like(tot)
    work(key_mean(q), last, (side(1 - core), 2), sems, q, kc, vc, acc, tot)
    for copy in state:
        copy.wait()
    acc[...] += acc0[...]
    tot[...] += tot0[...]
    total = jnp.sum(tot[...], axis=1, keepdims=True)
    out[:, :T] = (acc[...] * (1.0 / total)).astype(jnp.bfloat16).reshape(SRC, T, HD)
    tail = tail_rows(key_mean(q), TAIL)
    out[:, T:] = jnp.broadcast_to(tail[None], (SRC, TAIL, HD))
    fine = jnp.where((total > LOW) & (total < HIGH), 0.0, 1.0)

    @pl.when(jnp.max(fine) > 0.0)
    def _():
        near, away = side(core), side(1 - core)
        srcs = [(o0, 0, 0), (o1, 0, 1), (m0, near, 0), (s1, away, 1)]
        srcs += [(m1, near, 1), (f0, 2, 0), (s0, away, 0), (f1, 2, 1)]
        robust(q, srcs, out, acc, acc0, tot, stage)


STATE = jax.ShapeDtypeStruct((ROWS, HD), jnp.float32)


def call(kernel, name, ins, outs, scratch, units):
    return functools.partial(
        pl.pallas_call(
            kernel,
            name=name,
            in_specs=ins,
            out_specs=[VMEM] * len(outs),
            out_shape=outs,
            scratch_shapes=scratch,
            compiler_params=pltpu.CompilerParams(vmem_limit_bytes=VMEM_BYTES),
            cost_estimate=pl.CostEstimate(
                flops=units * 32 * G * 2 * G * HD, bytes_accessed=4 << 20, transcendentals=0
            ),
        )
    )


def shards(queries, keys, values):
    def by_head(a):
        return a.reshape(T, SRC, HD).transpose(1, 0, 2)

    def exchange(a):
        return lax.all_to_all(a, ("z", "y"), 0, 0, tiled=True)

    right = [(i, (i + 1) % NX) for i in range(NX)]
    left = [(i, (i - 1) % NX) for i in range(NX)]
    across = [(i, (i + 2) % NX) for i in range(NX)]
    swap = [(0, 1), (1, 0)]
    kv = jnp.stack([by_head(keys), by_head(values)], axis=1)
    with jax.named_scope("kv_to_heads"):
        own = exchange(kv)
    with jax.named_scope("key_sums"):
        sums = jnp.sum(keys.astype(jnp.float32), axis=0).reshape(SRC, HD)
        sums = sums + lax.ppermute(sums, "core", swap)
        sums = sums + sum(lax.ppermute(sums, "x", p) for p in (right, left, across))
        high = lax.reduce_precision(sums, 8, 7)
        mid = lax.reduce_precision(sums - high, 8, 7)
        parts = jnp.stack([high, mid, sums - high - mid], axis=1).astype(jnp.bfloat16)
        parts = jnp.pad(parts, ((0, 0), (0, TAIL - 3), (0, 0)))
    queries, parts, own = lax.optimization_barrier((queries, parts, own))
    with jax.named_scope("q_to_heads"):
        q = exchange(jnp.concatenate([by_head(queries), parts], axis=1))
    ring = [(NC * i, NC * j) for i, j in right] + [(NC * i + 1, NC * j + 1) for i, j in left]
    with jax.named_scope("ring"):
        m0 = lax.ppermute(own, ("x", "core"), ring)
        o1 = lax.ppermute(own, "core", swap)
        m1 = lax.ppermute(o1, ("x", "core"), ring)
        s1 = lax.ppermute(m0, "core", swap)
        s1, q = lax.optimization_barrier((s1, q))
        f0 = lax.ppermute(m0, ("x", "core"), ring)

    def bufs(ns):
        return [pltpu.VMEM((NZ, ns, NY, T, HD), jnp.bfloat16)] * 2 + [
            pltpu.SemaphoreType.DMA((NZ,))
        ]

    state = [pltpu.VMEM((ROWS, HD), jnp.float32)] * 2
    first = [VMEM] + [ANY] * 4
    acc, tot = call(first_kernel, "first", first, [STATE] * 2, bufs(4), 76)(q, own, o1, m0, s1)
    m1, f0, acc, tot = lax.optimization_barrier((m1, f0, acc, tot))
    with jax.named_scope("ring"):
        s0 = lax.ppermute(m1, "core", swap)
        f1 = lax.ppermute(f0, "core", swap)
    acc, tot = call(
        second_kernel,
        "second",
        first,
        [STATE] * 2,
        bufs(2) + state + [pltpu.SemaphoreType.DMA((2,))],
        36,
    )(q, m1, f0, acc, tot)
    (out,) = call(
        third_kernel,
        "third",
        [VMEM] + [ANY] * 10,
        [jax.ShapeDtypeStruct((SRC, T + TAIL, HD), jnp.bfloat16)],
        state
        + bufs(2)
        + state
        + [pltpu.SemaphoreType.DMA((2,)), pltpu.VMEM((SRC, 2, T, HD), jnp.bfloat16)],
        36,
    )(q, s0, f1, acc, tot, own, o1, m0, s1, m1, f0)
    with jax.named_scope("home"):
        home = exchange(out)
    attended = home[:, :T].transpose(1, 0, 2).reshape(T, SRC * HD)
    parts = home[:, T : T + 3].astype(jnp.float32)
    mean = (parts[:, 0] + parts[:, 1] + parts[:, 2]).reshape(SRC * HD)
    key_cache = (keys.astype(jnp.float32) - mean).astype(jnp.bfloat16)
    return attended, key_cache


def solution(mesh):
    split = Mesh(mesh.devices.reshape(NZ, NX, NY, NC), ALL)
    spec = P(ALL, None)
    return jax.shard_map(
        shards, mesh=split, in_specs=(spec,) * 3, out_specs=(spec,) * 2, check_vma=False
    )
```
